128 devices in a mesh: section: 4 (over z_lo, core), expert: 32 (over y, z_hi, x).
Axes of the slice: x: 4, y: 4, z: 4 (z_hi: 2, z_lo: 2; z = z_hi * 2 + z_lo), core: 2. Of those that a mesh axis runs over, the one named last changes fastest.
Arguments:
- tokens: bfloat16 [8, 512, 2048], P(None, 'expert'), may hold values from -6 to 6
- cotangent: bfloat16 [8, 512, 2048], P(None, 'expert'), may hold values from -6 to 6
- reward_weight: float32 [8, 512], P(None, 'expert'), may hold values from 0.2 to 14, as said below
- routes: int32 [4, 8, 512, 8], P('section', None, 'expert'), may hold values from 0 to 31, all different within a row; in each aligned block of 16 rows (0 to 15, 16 to 31, ..., all dimensions but the last counted through in order) at most 5 rows name the same one
- combine: float32 [4, 8, 512, 8], P('section', None, 'expert'), may hold values from 0.05 to 0.25
- w_up: bfloat16 [4, 32, 2048, 768], P('section', 'expert'), may hold values from -0.125 to 0.125
- w_down: bfloat16 [4, 32, 768, 2048], P('section', 'expert'), may hold values from -0.21875 to 0.21875
Outputs:
- layer_out: bfloat16 [4, 8, 512, 2048], P('section', None, 'expert')
- input_grad: bfloat16 [4, 8, 512, 2048], P('section', None, 'expert')
- grad_up: bfloat16 [4, 32, 2048, 768], P('section', 'expert')
The draws below stay inside these ranges and needn't reach their ends.
Inputs may be any that keep to these rules, and one draw needn't show every extreme that they name: `routes`: each row names 8 different experts. Within the 16 rows of one device for one layer and micro-batch, no expert is named more than 5 times. `reward_weight`: Positive.
All inputs are finite; a program needn't handle non-finite values.
Results may differ from the reference program's by a relative error of at most 0.018.
Values may be sent and summed in bfloat16 or wider, within the bound.
A program may use at most 192 MiB of HBM per device.

```python
import math
import jax
import jax.numpy as jnp
import numpy as np
from jax import lax

D = 2048
FF = 768
TOP = 8
MICRO = 8
TOK_DEV = 16
EXPERTS = 32
TOKENS = 512
CAP = 5
N_SECTION = 4
N_EXPERT = 32


def draw_reward_weight(key, part):
    position = jnp.arange(TOKENS, dtype=jnp.float32) / TOKENS
    rising = 1.0 + 2.0 * position
    spread = jax.random.uniform(key, (MICRO, TOKENS), jnp.float32, -1.5, 1.5)
    return jnp.exp(spread) * rising[None, :]


def level_of(rng, shape, cuts, least, top_value):
    gain = 1.0
    for dim, blocks in cuts:
        steps = jax.random.uniform(jax.random.fold_in(jax.random.fold_in(rng, 6), dim), (blocks,), jnp.float32, least / len(cuts), top_value / len(cuts))
        gain = gain * jnp.repeat(jnp.exp(steps), shape[dim] // blocks).reshape((-1,) + (1,) * (len(shape) - 1 - dim))
    return gain


def routed_block(key, own, number, rows, amount, top, reach, slope):
    ranking = jax.random.permutation(key, amount)
    packed, common = shares(amount, rows * top, reach, slope, True), shares(amount, rows * top, reach, slope, False)
    places = jnp.arange(amount)

    def named(tallies, turn):
        used = int((tallies > 0).sum())
        fixed = max(1, used // 4)
        passed = fixed + (places - fixed + turn * (used - fixed)) % max(1, amount - fixed)
        return jnp.zeros((amount,), jnp.int32).at[ranking[jnp.where(places < fixed, places, passed)]].set(jnp.asarray(tallies, jnp.int32))

    tallies = jnp.where(number % 4 == 0, named(packed, number // 4), named(common, number - number // 4 - 1))
    mixed = jax.random.permutation(jax.random.fold_in(own, 3), amount)
    source_of, taker = mixed[0:amount // 2 * 2:2], mixed[1:amount // 2 * 2:2]
    slack = jnp.minimum(tallies[source_of] - 1, reach - tallies[taker]) // 2
    slack = jnp.where((source_of == ranking[0]) | (taker == ranking[0]) | (tallies[taker] == 0), 0, jnp.maximum(slack, 0))
    passed = jax.random.randint(jax.random.fold_in(own, 4), (amount // 2,), 0, 1 << 20) % (slack + 1)
    tallies = tallies.at[source_of].add(-passed).at[taker].add(passed)
    items = jnp.searchsorted(jnp.cumsum(tallies), jnp.arange(rows * top), side="right").astype(jnp.int32)
    grid = items.reshape(top, rows).T
    grid = grid[jax.random.permutation(jax.random.fold_in(own, 1), rows)]
    turn = jax.random.randint(jax.random.fold_in(own, 2), (rows, 1), 0, top)
    return jnp.take_along_axis(grid, (jnp.arange(top)[None, :] + turn) % top, axis=1)


def shares(amount, total, most, slope, full):
    portions = [(1 << 20) // math.isqrt(rank ** slope) + 1 for rank in range(1, amount + 1)]
    largest = most if full else min(most, max(-(-total // amount), total * portions[0] // sum(portions)))
    least = 1 if total - largest >= amount - 1 else 0
    counts, surplus = [largest] + [least] * (amount - 1), total - largest - least * (amount - 1)
    while surplus > 0:
        candidates = [i for i in range(1, amount) if counts[i] < largest] or [i for i in range(1, amount) if counts[i] < most]
        mass, remaining = sum([portions[i] for i in candidates]), surplus
        for i in candidates:
            extra = min(most - counts[i], max(1, remaining * portions[i] // mass), surplus)
            counts[i] = counts[i] + extra
            surplus = surplus - extra
    return np.array(counts)


def scatter_about(stream_key, shape, deviation, most, split=(), kind=jnp.bfloat16):
    entries = deviation * jax.random.normal(stream_key, shape, jnp.float32)
    if split:
        entries = entries * level_of(stream_key, shape, split, -0.22, 0.18)
    return jnp.clip(entries, -most, most).astype(kind)


def setup_inputs(seed: int = 0) -> dict:
    splits = jax.random.split(jax.random.key(seed), 8)
    tokens = scatter_about(splits[0], (MICRO, TOKENS, D), 1.0, 6.0, ((1, 32),))
    cotangent = scatter_about(splits[1], (MICRO, TOKENS, D), 1.0, 6.0, ((1, 32),))
    reward_weight = draw_reward_weight(jax.random.fold_in(splits[7], 71), 0)
    routes_keys = jax.random.split(jax.random.fold_in(splits[3], 1), N_SECTION * MICRO * TOKENS // TOK_DEV)
    routes_turns = jax.random.permutation(jax.random.fold_in(splits[3], 3), N_SECTION * MICRO * TOKENS // TOK_DEV)
    routes = jax.vmap(lambda own, number: routed_block(jax.random.fold_in(splits[3], 2), own, number, TOK_DEV, EXPERTS, TOP, CAP, 2))(routes_keys, routes_turns).reshape((N_SECTION, MICRO, TOKENS, TOP))
    combine = jnp.clip(0.05 + 0.2 * jax.random.uniform(splits[4], (N_SECTION, MICRO, TOKENS, TOP), jnp.float32) ** level_of(splits[4], (N_SECTION, MICRO, TOKENS, TOP), ((0, 4), (2, 32)), -0.2, 0.2), 0.05, 0.25)
    w_up = scatter_about(splits[5], (N_SECTION, EXPERTS, D, FF), D ** -0.5, 0.125, ((0, 4), (1, 32)))
    w_down = scatter_about(splits[6], (N_SECTION, EXPERTS, FF, D), FF ** -0.5, 0.21875, ((0, 4), (1, 32)))
    return {"tokens": tokens, "cotangent": cotangent, "reward_weight": reward_weight, "routes": routes, "combine": combine, "w_up": w_up, "w_down": w_down}


EPS = 1e-06

def rms_forward(inputs):
    values = inputs.astype(jnp.float32)
    scale = lax.rsqrt(lax.optimization_barrier(jnp.mean(values * values, axis=-1, keepdims=True)) + EPS)
    return values * scale

def rms_backward(inputs, grad):
    values = inputs.astype(jnp.float32)
    scale = lax.rsqrt(lax.optimization_barrier(jnp.mean(values * values, axis=-1, keepdims=True)) + EPS)
    inner = lax.optimization_barrier(jnp.mean(grad * values, axis=-1, keepdims=True))
    return scale * grad - values * (scale * scale * scale) * inner

def silu_slope(pre):
    sigma = jax.nn.sigmoid(pre)
    return sigma * (1.0 + pre * (1.0 - sigma))

def layer_slots(route):
    blocks = route.reshape(N_EXPERT, TOK_DEV * TOP).astype(jnp.int32)
    onehot = (blocks[:, :, None] == jnp.arange(EXPERTS, dtype=jnp.int32)[None, None, :]).astype(jnp.int32)
    before = jnp.cumsum(onehot, axis=1) - onehot
    rank = lax.optimization_barrier(jnp.sum(before * onehot, axis=2))
    source = jnp.arange(N_EXPERT, dtype=jnp.int32)[:, None]
    return (blocks * (N_EXPERT * CAP) + source * CAP + rank).reshape(-1).astype(jnp.int32)

def expert_inputs(x_in, slot):
    pair_token = jnp.arange(TOKENS * TOP, dtype=jnp.int32) // TOP
    normed = rms_forward(x_in).astype(jnp.bfloat16)
    buffer = jnp.zeros((EXPERTS * N_EXPERT * CAP, D), jnp.bfloat16).at[slot].set(normed[pair_token])
    return buffer.reshape(EXPERTS, N_EXPERT * CAP, D)

def forward_layer(x_in, route, coef, up, down):
    slot = layer_slots(route)
    buffer = expert_inputs(x_in, slot)
    pre = jnp.einsum('erd,edf->erf', buffer.astype(jnp.float32), up.astype(jnp.float32))
    act = jax.nn.silu(pre).astype(jnp.bfloat16)
    result = jnp.einsum('erf,efd->erd', act.astype(jnp.float32), down.astype(jnp.float32)).astype(jnp.bfloat16)
    rows = result.reshape(-1, D)[slot].astype(jnp.float32)
    mixed = (rows * coef.reshape(-1)[:, None]).reshape(TOKENS, TOP, D).sum(axis=1)
    return (x_in.astype(jnp.float32) + mixed).astype(jnp.bfloat16)

def backward_layer(x_in, grad, route, coef, up, down):
    slot = layer_slots(route)
    pair_token = jnp.arange(TOKENS * TOP, dtype=jnp.int32) // TOP
    buffer = expert_inputs(x_in, slot)
    pre = jnp.einsum('erd,edf->erf', buffer.astype(jnp.float32), up.astype(jnp.float32))
    scaled = (grad.astype(jnp.float32)[pair_token] * coef.reshape(-1)[:, None]).astype(jnp.bfloat16)
    grad_buffer = jnp.zeros((EXPERTS * N_EXPERT * CAP, D), jnp.bfloat16).at[slot].set(scaled)
    grad_buffer = grad_buffer.reshape(EXPERTS, N_EXPERT * CAP, D)
    grad_act = jnp.einsum('erd,efd->erf', grad_buffer.astype(jnp.float32), down.astype(jnp.float32))
    grad_pre = (grad_act * silu_slope(pre)).astype(jnp.bfloat16)
    term = jnp.einsum('erd,erf->edf', buffer.astype(jnp.float32), grad_pre.astype(jnp.float32))
    grad_rows = jnp.einsum('erf,edf->erd', grad_pre.astype(jnp.float32), up.astype(jnp.float32)).astype(jnp.bfloat16)
    gathered = grad_rows.reshape(-1, D)[slot].astype(jnp.float32)
    grad_normed = gathered.reshape(TOKENS, TOP, D).sum(axis=1)
    grad_x = (grad.astype(jnp.float32) + rms_backward(x_in, grad_normed)).astype(jnp.bfloat16)
    return (grad_x, term)

def reference(tokens, cotangent, reward_weight, routes, combine, w_up, w_down):
    inputs_kept = []
    outputs = []
    current = [tokens[m] for m in range(MICRO)]
    for layer in range(N_SECTION):
        inputs_kept.append(current)
        nxt = [forward_layer(current[m], routes[layer, m], combine[layer, m], w_up[layer], w_down[layer]) for m in range(MICRO)]
        outputs.append(jnp.stack(nxt))
        current = nxt
    total = jnp.sum(reward_weight)
    factor = reward_weight * (MICRO * TOKENS / total)
    grads = [(cotangent[m].astype(jnp.float32) * factor[m][:, None]).astype(jnp.bfloat16) for m in range(MICRO)]
    input_grads = [None] * N_SECTION
    weight_grads = [None] * N_SECTION
    for layer in range(N_SECTION - 1, -1, -1):
        acc = jnp.zeros((EXPERTS, D, FF), jnp.float32)
        new_grads = []
        for m in range(MICRO):
            grad_x, term = backward_layer(inputs_kept[layer][m], grads[m], routes[layer, m], combine[layer, m], w_up[layer], w_down[layer])
            acc = acc + term
            new_grads.append(grad_x)
        input_grads[layer] = jnp.stack(new_grads)
        weight_grads[layer] = acc.astype(jnp.bfloat16)
        grads = new_grads
    return (jnp.stack(outputs), jnp.stack(input_grads), jnp.stack(weight_grads))
```

```python
import functools

import jax
import jax.numpy as jnp
from jax import lax
from jax.experimental import pallas as pl
from jax.experimental.pallas import tpu as pltpu
from jax.sharding import PartitionSpec as P

EPS = 1e-06
MESH = pl.DeviceIdType.MESH
BF = jnp.bfloat16
F32 = jnp.float32

PEERS = 32
CAP = 5
ROWS = PEERS * CAP
TOK = 16
TOP = 8
MICRO = 8
OWN = 4
D = 2048
FF = 768
SUB = 16
PAIRS = TOK * TOP
TAB = 384


def kernel(
    tok_hbm, cot_hbm, up_hbm, dn_hbm, it_hbm, ft_hbm, rloc_hbm, rw,
    lo_hbm, ig_hbm, gu_hbm,
    wup, wdn, rows, pre, gp, recv_a, recv_b, recv_d, send_a, send_b, work, nrm, gb, act, lay,
    gpart, grecv, xbuf, gbuf, itv, ftv, its, fts, rsum,
    wsem, wssem, tsem, tssem, ssem_t, rsem, rssem, asem, bsem, dsem, esem, ssa, ssb,
    insem, xsem, gsem, xs, osem, orsem, ossem, gusem, gssem,
):
    sec = lax.axis_index("section")
    me = lax.axis_index("expert")
    chip = sec // 2
    core = lax.rem(sec, 2)
    other = chip * 2 + (1 - core)
    across = (1 - chip) * 2 + core
    diag = (1 - chip) * 2 + (1 - core)

    pltpu.make_async_copy(up_hbm, wup.at[core], wsem.at[core, 0]).start()
    pltpu.make_async_copy(dn_hbm, wdn.at[core], wsem.at[core, 1]).start()
    pltpu.make_async_copy(it_hbm, itv.at[sec], tsem.at[0, sec]).start()
    pltpu.make_async_copy(ft_hbm, ftv.at[sec], tsem.at[1, sec]).start()

    def load_tokens(j, _):
        @pl.when(chip == 0)
        def _():
            pltpu.make_async_copy(tok_hbm.at[2 * j + core], xbuf.at[j, 0], insem.at[j]).start()

        @pl.when(chip == 1)
        def _():
            pltpu.make_async_copy(cot_hbm.at[2 * j + core], gbuf.at[j, 2], insem.at[j]).start()

        return 0

    lax.fori_loop(0, OWN, load_tokens, 0)

    barrier = pltpu.get_barrier_semaphore()

    def greet(i, _):
        p = lax.rem(me + 1 + i, PEERS)

        @pl.when(p != me)
        def _():
            pl.semaphore_signal(barrier, inc=1, device_id=(sec, p), device_id_type=MESH)

        pl.semaphore_signal(barrier, inc=1, device_id=(across, p), device_id_type=MESH)
        return 0

    lax.fori_loop(0, PEERS, greet, 0)
    pl.semaphore_signal(barrier, inc=1, device_id=(other, me), device_id_type=MESH)
    pl.semaphore_signal(barrier, inc=1, device_id=(diag, me), device_id_type=MESH)
    pl.semaphore_wait(barrier, 2 * PEERS + 1)

    for n, far in enumerate((other, across, diag)):
        pltpu.make_async_remote_copy(
            it_hbm, itv.at[sec], tssem.at[0, n], tsem.at[0, sec], device_id=(far, me), device_id_type=MESH
        ).start()
        pltpu.make_async_remote_copy(
            ft_hbm, ftv.at[sec], tssem.at[1, n], tsem.at[1, sec], device_id=(far, me), device_id_type=MESH
        ).start()

    @pl.when(chip == 1)
    def _():
        pltpu.make_async_copy(rloc_hbm, rsum.at[me], rsem).start()

        def send_sum(i, _):
            p = lax.rem(me + 1 + i, PEERS)
            pltpu.make_async_remote_copy(
                rloc_hbm, rsum.at[me], rssem, rsem, device_id=(sec, p), device_id_type=MESH
            ).start()
            return 0

        lax.fori_loop(0, PEERS - 1, send_sum, 0)

    w_up_far = pltpu.make_async_remote_copy(
        up_hbm, wup.at[core], wssem.at[0], wsem.at[core, 0], device_id=(other, me), device_id_type=MESH
    )
    w_dn_far = pltpu.make_async_remote_copy(
        dn_hbm, wdn.at[core], wssem.at[1], wsem.at[core, 1], device_id=(other, me), device_id_type=MESH
    )
    w_up_far.start()
    w_dn_far.start()

    def tables_in(n, _):
        pltpu.make_async_copy(itv.at[n], itv.at[n], tsem.at[0, n]).wait()
        pltpu.make_async_copy(ftv.at[n], ftv.at[n], tsem.at[1, n]).wait()
        return 0

    lax.fori_loop(0, 4, tables_in, 0)
    c1 = pltpu.make_async_copy(itv, its, ssem_t.at[0])
    c2 = pltpu.make_async_copy(ftv, fts, ssem_t.at[1])
    c1.start()
    c2.start()
    c1.wait()
    c2.wait()

    def wait_weights(q):
        pltpu.make_async_copy(wup.at[q], wup.at[q], wsem.at[q, 0]).wait()
        pltpu.make_async_copy(wdn.at[q], wdn.at[q], wsem.at[q, 1]).wait()

    def dispatch(j, layer, recv, sem, scaled):
        here = layer // 2 == chip
        target = (layer // 2) * 2 + core
        unit = lax.rem(layer, 2) * OWN + j
        m = 2 * j + core

        def one(i, _):
            p = lax.rem(me + 1 + i, PEERS)
            for r in range(CAP):
                at = PAIRS + p * CAP + r
                row = nrm[its[layer, m, at]]
                if scaled:
                    row = (row.astype(F32) * fts[layer, m, at]).astype(BF)
                send_a[j, p, r] = row

            @pl.when(jnp.logical_not(jnp.logical_and(here, p == me)))
            def _():
                pltpu.make_async_remote_copy(
                    send_a.at[j, p], recv.at[unit, me], ssa.at[j], sem.at[unit],
                    device_id=(target, p), device_id_type=MESH,
                ).start()

            return 0

        lax.fori_loop(0, PEERS, one, 0)

        @pl.when(here)
        def _():
            recv[unit, me] = send_a[j, me]

    def wait_blocks(buffer, sem, far):
        most = buffer.at[pl.ds(0, PEERS - 1)]
        if far is False:
            pltpu.make_async_copy(most, most, sem).wait()
            return

        @pl.when(far)
        def _():
            pltpu.make_async_copy(buffer, buffer, sem).wait()

        @pl.when(jnp.logical_not(far))
        def _():
            pltpu.make_async_copy(most, most, sem).wait()

    def wait_dispatch(j, far):
        wait_blocks(send_a.at[j], ssa.at[j], far)

    def normed(value):
        v = value.astype(F32)
        mean = jnp.sum(v * v, axis=(0, 1), keepdims=True) * (1.0 / D)
        return (v * lax.rsqrt(mean + EPS)).astype(BF)

    def first_forward(j, _):
        pltpu.make_async_copy(xbuf.at[j, 0], xbuf.at[j, 0], insem.at[j]).wait()

        def one(t, _):
            nrm[t] = normed(xbuf[j, 0, t])
            return 0

        lax.fori_loop(0, TOK, one, 0, unroll=4)
        dispatch(j, 0, recv_a, asem, False)
        return 0

    def first_backward(j, _):
        pltpu.make_async_copy(gbuf.at[j, 2], gbuf.at[j, 2], insem.at[j]).wait()
        total = jnp.sum(rsum[...], axis=0)
        inverse = (MICRO * TOK * PEERS) / total
        m = 2 * j + core

        def one(t, _):
            factor = rw[m, t] * inverse[0:1, :]
            g = (gbuf[j, 2, t].astype(F32) * factor).astype(BF)
            gbuf[j, 2, t] = g
            nrm[t] = g
            return 0

        lax.fori_loop(0, TOK, one, 0, unroll=4)
        dispatch(j, 3, recv_d, dsem, True)
        return 0

    @pl.when(chip == 0)
    def _():
        lax.fori_loop(0, 2, first_forward, 0)

    @pl.when(chip == 1)
    def _():
        pltpu.make_async_copy(rsum, rsum, rsem).wait()
        lax.fori_loop(0, OWN, first_backward, 0)
        pltpu.make_async_copy(rsum.at[pl.ds(0, PEERS - 1)], rsum.at[pl.ds(0, PEERS - 1)], rssem).wait()

    wait_weights(0)

    def flatten(recv, unit, dst, *lead):
        for n in range(PEERS):
            lay[pl.ds(n * CAP * SUB, CAP * SUB), :] = (
                recv[unit, n].astype(F32).reshape(CAP * SUB, 128)
            )
        for n in range(ROWS // SUB):
            for b in range(SUB):
                part = lay[pl.ds(n * SUB * SUB + b, SUB, stride=SUB), :]
                if lead:
                    q, start = lead
                    dst[q, pl.ds(pl.multiple_of(start + n * SUB, SUB), SUB), pl.ds(b * 128, 128)] = part.astype(BF)
                else:
                    dst[pl.ds(n * SUB, SUB), pl.ds(b * 128, 128)] = part.astype(BF)

    def put_back(n, tile):
        for h in range(2):
            lay[pl.ds(2 * n + h, ROWS, stride=SUB), :] = tile[:, h * 128:(h + 1) * 128]

    def give_back(slot, unit, sem, again):
        @pl.when(again)
        def _():
            pltpu.make_async_copy(
                send_b.at[slot, pl.ds(0, PEERS - 1)], send_b.at[slot, pl.ds(0, PEERS - 1)], ssb.at[slot]
            ).wait()

        def one(i, _):
            p = lax.rem(me + 1 + i, PEERS)
            at = pl.multiple_of(p * (CAP * SUB), CAP * SUB)
            send_b[slot, p] = lay[pl.ds(at, CAP * SUB), :].reshape(CAP, SUB, 128).astype(BF)

            @pl.when(p != me)
            def _():
                pltpu.make_async_remote_copy(
                    send_b.at[slot, p], recv_b.at[unit, me], ssb.at[slot], sem.at[unit],
                    device_id=(sec, p), device_id_type=MESH,
                ).start()

            return 0

        lax.fori_loop(0, PEERS, one, 0)
        recv_b[unit, me] = send_b[slot, me]

    def expert_forward(j, q, slot, again):
        unit = q * OWN + j
        start = pl.multiple_of(j * ROWS, ROWS)
        wait_blocks(recv_a.at[unit], asem.at[unit], jnp.logical_and(chip == 1, q == 0))
        flatten(recv_a, unit, rows, q, start)
        span = pl.ds(start, ROWS)
        for n in range(FF // 256):
            cols = pl.ds(n * 256, 256)
            v = jnp.dot(rows[q, span, :], wup[q, :, cols], preferred_element_type=F32)
            pre[q, span, cols] = v
            act[:, cols] = (v * jax.nn.sigmoid(v)).astype(BF)
        for n in range(D // 256):
            put_back(n, jnp.dot(act[...], wdn[q, :, pl.ds(n * 256, 256)], preferred_element_type=F32))
        give_back(slot, unit, bsem, again)

    contract_last = (((1,), (1,)), ((), ()))

    def expert_backward(j, q, slot):
        unit = q * OWN + j
        start = pl.multiple_of(j * ROWS, ROWS)
        wait_blocks(recv_d.at[unit], dsem.at[unit], jnp.logical_and(chip == 0, q == 1))
        flatten(recv_d, unit, gb)
        span = pl.ds(start, ROWS)
        for n in range(FF // 256):
            cols = pl.ds(n * 256, 256)
            v = lax.dot_general(gb[...], wdn[q, cols, :], contract_last, preferred_element_type=F32)
            h = pre[q, span, cols]
            s = jax.nn.sigmoid(h)
            gp[q, span, cols] = (v * (s * (1.0 + h * (1.0 - s)))).astype(BF)
        for n in range(D // 256):
            put_back(
                n,
                lax.dot_general(
                    gp[q, span, :], wup[q, pl.ds(n * 256, 256), :], contract_last, preferred_element_type=F32
                ),
            )
        give_back(slot, unit, esem, True)

    def copy_out(kind, j, q, src, dst_hbm):
        m = 2 * j + core

        @pl.when(q == core)
        def _():
            pltpu.make_async_copy(src, dst_hbm.at[m], osem.at[kind, j]).start()

        @pl.when(q != core)
        def _():
            pltpu.make_async_remote_copy(
                src, dst_hbm.at[m], ossem.at[kind, j], orsem.at[kind, j],
                device_id=(other, me), device_id_type=MESH,
            ).start()

    def home_forward(j, q):
        unit = q * OWN + j
        layer = 2 * chip + q
        m = 2 * j + core

        @pl.when(jnp.logical_and(chip == 1, q == 0))
        def _():
            pltpu.make_async_copy(xbuf.at[j, 0], xbuf.at[j, 0], xsem.at[j]).wait()

        wait_blocks(recv_b.at[unit], bsem.at[unit], False)
        work[...] = recv_b[unit].reshape(ROWS, SUB, 128)

        def one(t, _):
            total = xbuf[j, q, t].astype(F32)
            for n in range(TOP):
                total += fts[layer, m, t * TOP + n] * work[its[layer, m, t * TOP + n]].astype(F32)
            out = total.astype(BF)
            xbuf[j, q + 1, t] = out
            nrm[t] = normed(out)
            return 0

        lax.fori_loop(0, TOK, one, 0, unroll=4)

        @pl.when(jnp.logical_not(jnp.logical_and(chip == 1, q == 1)))
        def _():
            wait_dispatch(j, False)
            dispatch(j, layer + 1, recv_a, asem, False)

        @pl.when(jnp.logical_and(chip == 0, q == 1))
        def _():
            pltpu.make_async_remote_copy(
                xbuf.at[j, 2], xbuf.at[j, 0], xs.at[j], xsem.at[j],
                device_id=(across, me), device_id_type=MESH,
            ).start()

        copy_out(0, j, q, xbuf.at[j, q + 1], lo_hbm)

    def home_backward(j, q):
        unit = q * OWN + j
        layer = 2 * chip + q
        m = 2 * j + core

        @pl.when(jnp.logical_and(chip == 0, q == 1))
        def _():
            pltpu.make_async_copy(gbuf.at[j, 2], gbuf.at[j, 2], gsem.at[j]).wait()

        wait_blocks(recv_b.at[unit], esem.at[unit], False)
        work[...] = recv_b[unit].reshape(ROWS, SUB, 128)

        def one(t, _):
            grad = work[its[layer, m, t * TOP]].astype(F32)
            for n in range(1, TOP):
                grad += work[its[layer, m, t * TOP + n]].astype(F32)
            x = xbuf[j, q, t].astype(F32)
            scale = lax.rsqrt(jnp.sum(x * x, axis=(0, 1), keepdims=True) * (1.0 / D) + EPS)
            inner = jnp.sum(grad * x, axis=(0, 1), keepdims=True) * (1.0 / D)
            g = gbuf[j, q + 1, t].astype(F32)
            out = (g + (scale * grad - x * (scale * scale * scale) * inner)).astype(BF)
            gbuf[j, q, t] = out
            nrm[t] = out
            return 0

        lax.fori_loop(0, TOK, one, 0, unroll=4)

        @pl.when(jnp.logical_not(jnp.logical_and(chip == 0, q == 0)))
        def _():
            wait_dispatch(j, chip == 0)
            dispatch(j, layer - 1, recv_d, dsem, True)

        @pl.when(jnp.logical_and(chip == 1, q == 0))
        def _():
            pltpu.make_async_remote_copy(
                gbuf.at[j, 0], gbuf.at[j, 2], xs.at[j], gsem.at[j],
                device_id=(across, me), device_id_type=MESH,
            ).start()

        copy_out(1, j, q, gbuf.at[j, q], ig_hbm)

    def forward_step(step, _):
        pair, q = step // 2, lax.rem(step, 2)

        @pl.when(step == 1)
        def _():
            wait_weights(1)

        def run(i, _):
            expert_forward(2 * pair + i, q, i, step > 0)
            return 0

        lax.fori_loop(0, 2, run, 0)

        @pl.when(jnp.logical_and(step == 0, chip == 0))
        def _():
            lax.fori_loop(2, OWN, first_forward, 0)

        def close(i, _):
            home_forward(2 * pair + i, q)
            return 0

        lax.fori_loop(0, 2, close, 0)
        return 0

    lax.fori_loop(0, 4, forward_step, 0)

    def weight_grad(q):
        def one(n, _):
            at = pl.multiple_of(n * 256, 256)
            gpart[q, pl.ds(at, 256), :] = lax.dot_general(
                rows[q, :, pl.ds(at, 256)], gp[q], (((0,), (0,)), ((), ())), preferred_element_type=F32
            ).astype(BF)
            return 0

        lax.fori_loop(0, D // 256, one, 0)

    def backward_step(step, _):
        pair, q = step // 2, 1 - lax.rem(step, 2)

        def run(i, _):
            expert_backward(2 * pair + i, q, i)
            return 0

        lax.fori_loop(0, 2, run, 0)

        @pl.when(step >= 2)
        def _():
            weight_grad(q)

            @pl.when(q != core)
            def _():
                pltpu.make_async_remote_copy(
                    gpart.at[q], grecv, gssem, gusem.at[0], device_id=(other, me), device_id_type=MESH
                ).start()

        def close(i, _):
            home_backward(2 * pair + i, q)
            return 0

        lax.fori_loop(0, 2, close, 0)
        return 0

    lax.fori_loop(0, 4, backward_step, 0)

    pltpu.make_async_copy(grecv, grecv, gusem.at[0]).wait()

    def add(n, _):
        at = pl.ds(pl.multiple_of(n * 128, 128), 128)
        gpart[core, at, :] = (gpart[core, at, :].astype(F32) + grecv[at, :].astype(F32)).astype(BF)
        return 0

    lax.fori_loop(0, D // 128, add, 0)
    last = pltpu.make_async_copy(gpart.at[core], gu_hbm, gusem.at[1])
    last.start()

    def drain(j, _):
        wait_dispatch(j, chip == 1)
        pltpu.make_async_copy(xbuf.at[j, 0], xbuf.at[j, 0], xs.at[j]).wait()
        for kind in range(2):
            for sem in (osem, orsem, ossem):
                pltpu.make_async_copy(xbuf.at[j, 0], xbuf.at[j, 0], sem.at[kind, j]).wait()
        return 0

    lax.fori_loop(0, OWN, drain, 0)
    for slot in range(2):
        pltpu.make_async_copy(
            send_b.at[slot, pl.ds(0, PEERS - 1)], send_b.at[slot, pl.ds(0, PEERS - 1)], ssb.at[slot]
        ).wait()
    pltpu.make_async_copy(grecv, grecv, gssem).wait()
    w_up_far.wait_send()
    w_dn_far.wait_send()
    for n in range(3):
        pltpu.make_async_copy(itv.at[0], itv.at[0], tssem.at[0, n]).wait()
        pltpu.make_async_copy(ftv.at[0], ftv.at[0], tssem.at[1, n]).wait()
    last.wait()


def tables(routes, combine):
    route = routes.reshape(MICRO, PAIRS)
    coef = combine.reshape(MICRO, PAIRS)
    place = jnp.arange(PAIRS, dtype=jnp.int32)
    same = (route[:, :, None] == route[:, None, :]) & (place[None, None, :] < place[None, :, None])
    slot = route * CAP + jnp.sum(same.astype(jnp.int32), axis=2)
    hit = slot[:, None, :] == jnp.arange(ROWS, dtype=jnp.int32)[None, :, None]
    token = jnp.sum(jnp.where(hit, (place // TOP)[None, None, :], 0), axis=2)
    weight = jnp.sum(jnp.where(hit, coef[:, None, :], 0.0), axis=2)
    rest = TAB - PAIRS - ROWS
    ints = jnp.concatenate([slot, token, jnp.zeros((MICRO, rest), jnp.int32)], axis=1)
    floats = jnp.concatenate([coef, weight, jnp.zeros((MICRO, rest), F32)], axis=1)
    return ints, floats


def shards(tokens, cotangent, reward_weight, routes, combine, w_up, w_down):
    ints, floats = tables(routes[0], combine[0])
    local = jnp.broadcast_to(jnp.sum(reward_weight), (8, 128))
    blocks = (MICRO, TOK, SUB, 128)
    exchange = (PEERS, CAP, SUB, 128)
    anywhere = pl.BlockSpec(memory_space=pl.ANY)
    dma = pltpu.SemaphoreType.DMA
    lo, ig, gu = pl.pallas_call(
        kernel,
        out_shape=(
            jax.ShapeDtypeStruct(blocks, BF),
            jax.ShapeDtypeStruct(blocks, BF),
            jax.ShapeDtypeStruct((D, FF), BF),
        ),
        in_specs=[anywhere] * 7 + [pl.BlockSpec(memory_space=pltpu.SMEM)],
        out_specs=(anywhere,) * 3,
        scratch_shapes=[
            pltpu.VMEM((2, D, FF), BF),
            pltpu.VMEM((2, FF, D), BF),
            pltpu.VMEM((2, OWN * ROWS, D), BF),
            pltpu.VMEM((2, OWN * ROWS, FF), F32),
            pltpu.VMEM((2, OWN * ROWS, FF), BF),
            pltpu.VMEM((2 * OWN,) + exchange, BF),
            pltpu.VMEM((2 * OWN,) + exchange, BF),
            pltpu.VMEM((2 * OWN,) + exchange, BF),
            pltpu.VMEM((OWN,) + exchange, BF),
            pltpu.VMEM((2,) + exchange, BF),
            pltpu.VMEM((ROWS, SUB, 128), BF),
            pltpu.VMEM((TOK, SUB, 128), BF),
            pltpu.VMEM((ROWS, D), BF),
            pltpu.VMEM((ROWS, FF), BF),
            pltpu.VMEM((ROWS * SUB, 128), F32),
            pltpu.VMEM((2, D, FF), BF),
            pltpu.VMEM((D, FF), BF),
            pltpu.VMEM((OWN, 3, TOK, SUB, 128), BF),
            pltpu.VMEM((OWN, 3, TOK, SUB, 128), BF),
            pltpu.VMEM((4, MICRO, TAB), jnp.int32),
            pltpu.VMEM((4, MICRO, TAB), F32),
            pltpu.SMEM((4, MICRO, TAB), jnp.int32),
            pltpu.SMEM((4, MICRO, TAB), F32),
            pltpu.VMEM((PEERS, 8, 128), F32),
            dma((2, 2)), dma((2,)), dma((2, 4)), dma((2, 3)), dma((2,)), dma, dma,
            dma((2 * OWN,)), dma((2 * OWN,)), dma((2 * OWN,)), dma((2 * OWN,)), dma((OWN,)), dma((2,)),
            dma((OWN,)), dma((OWN,)), dma((OWN,)), dma((OWN,)),
            dma((2, OWN)), dma((2, OWN)), dma((2, OWN)), dma((2,)), dma,
        ],
        compiler_params=pltpu.CompilerParams(
            collective_id=0, has_side_effects=True, vmem_limit_bytes=62 * 1024 * 1024
        ),
        cost_estimate=pl.CostEstimate(
            flops=2 * 5 * MICRO * ROWS * D * FF, bytes_accessed=16 * 2**20, transcendentals=2 * MICRO * ROWS * FF
        ),
    )(
        tokens.reshape(blocks), cotangent.reshape(blocks), w_up[0, 0], w_down[0, 0], ints, floats, local, reward_weight
    )
    whole = (1, MICRO, TOK, D)
    return lo.reshape(whole), ig.reshape(whole), gu[None, None]


def solution(mesh):
    return jax.shard_map(
        shards,
        mesh=mesh,
        in_specs=(
            P(None, "expert", None),
            P(None, "expert", None),
            P(None, "expert"),
            P("section", None, "expert", None),
            P("section", None, "expert", None),
            P("section", "expert", None, None),
            P("section", "expert", None, None),
        ),
        out_specs=(
            P("section", None, "expert", None),
            P("section", None, "expert", None),
            P("section", "expert", None, None),
        ),
        check_vma=False,
    )
```

```python
import functools

import jax
import jax.numpy as jnp
from jax import lax
from jax.experimental import pallas as pl
from jax.experimental.pallas import tpu as pltpu
from jax.sharding import PartitionSpec as P

EPS = 1e-06
MESH = pl.DeviceIdType.MESH
BF = jnp.bfloat16
F32 = jnp.float32

PEERS = 32
CAP = 5
ROWS = PEERS * CAP
TOK = 16
TOP = 8
MICRO = 8
OWN = 4
D = 2048
FF = 768
SUB = 16
PAIRS = TOK * TOP
TAB = 384

FIRST, EXPERT_F, HOME_F, EXPERT_B, HOME_B, GRAD, WEIGHTS = range(7)


def steps(*words):
    names = {"I": FIRST, "X": EXPERT_F, "H": HOME_F, "Y": EXPERT_B, "G": HOME_B, "U": GRAD, "W": WEIGHTS}
    return [names[w[0]] * 8 + int(w[2]) * OWN + int(w[1]) for w in words]


ORDER = (
    steps(
        "I00", "I20", "I10", "W00", "X00", "X10", "H00", "H10", "W01", "X01",
        "X11", "H01", "H11", "I30", "X30", "X20", "H30", "H20", "X31", "X21",
        "H31", "H21", "Y11", "Y01", "G11", "G01", "Y10", "Y00", "G10", "G00",
        "Y31", "Y21", "G31", "U01", "G21", "Y30", "Y20", "U00", "G30", "G20",
    ),
    steps(
        "I30", "I20", "I10", "I00", "W00", "X00", "X10", "H00", "H10", "W01",
        "X01", "Y01", "X11", "Y11", "G01", "G11", "Y00", "X30", "X20", "Y10",
        "H30", "H20", "G10", "G00", "H11", "X31", "Y31", "X21", "Y21", "U01",
        "H31", "G31", "G21", "Y30", "Y20", "G30", "H01", "G20", "U00", "H21",
    ),
)


def kernel(
    tok_hbm, cot_hbm, up_hbm, dn_hbm, it_hbm, ft_hbm, rv, rw,
    lo_hbm, ig_hbm, own_hbm, far_hbm,
    wup, wdn, rows, pre, gp, recv_a, recv_b, recv_d, recv_e, send_a, send_b, work, nrm, gb, act, lay,
    gpart, inbuf, outbuf, xbuf, gbuf, itv, ftv, its, fts, rsum, rown,
    wsem, wssem, tsem, tssem, ssem_t, rsem, rssem, asem, bsem, dsem, esem, ssa, ssb,
    insem, xsem, gsem, xs, osem, orsem, ossem, gusem, gssem,
):
    sec = lax.axis_index("section")
    me = lax.axis_index("expert")
    chip = sec // 2
    core = lax.rem(sec, 2)
    other = chip * 2 + (1 - core)
    across = (1 - chip) * 2 + core
    diag = (1 - chip) * 2 + (1 - core)

    pltpu.make_async_copy(up_hbm, wup.at[core], wsem.at[core, 0]).start()
    pltpu.make_async_copy(dn_hbm, wdn.at[core], wsem.at[core, 1]).start()
    pltpu.make_async_copy(it_hbm, itv.at[sec], tsem.at[0, sec]).start()
    pltpu.make_async_copy(ft_hbm, ftv.at[sec], tsem.at[1, sec]).start()

    def load_tokens(j, _):
        @pl.when(chip == 0)
        def _():
            pltpu.make_async_copy(tok_hbm.at[2 * j + core], inbuf.at[j], insem.at[j]).start()

        @pl.when(chip == 1)
        def _():
            pltpu.make_async_copy(cot_hbm.at[2 * j + core], inbuf.at[j], insem.at[j]).start()

        return 0

    lax.fori_loop(0, OWN, load_tokens, 0)

    rown[...] = jnp.broadcast_to(jnp.sum(rv[...], axis=(0, 1), keepdims=True), (8, 128))

    barrier = pltpu.get_barrier_semaphore()

    def greet(i, _):
        p = lax.rem(me + 1 + i, PEERS)

        @pl.when(p != me)
        def _():
            pl.semaphore_signal(barrier, inc=1, device_id=(sec, p), device_id_type=MESH)

        pl.semaphore_signal(barrier, inc=1, device_id=(across, p), device_id_type=MESH)
        return 0

    lax.fori_loop(0, PEERS, greet, 0)
    pl.semaphore_signal(barrier, inc=1, device_id=(other, me), device_id_type=MESH)
    pl.semaphore_signal(barrier, inc=1, device_id=(diag, me), device_id_type=MESH)
    pl.semaphore_wait(barrier, 2 * PEERS + 1)

    for n, far in enumerate((other, across, diag)):
        pltpu.make_async_remote_copy(
            it_hbm, itv.at[sec], tssem.at[0, n], tsem.at[0, sec], device_id=(far, me), device_id_type=MESH
        ).start()
        pltpu.make_async_remote_copy(
            ft_hbm, ftv.at[sec], tssem.at[1, n], tsem.at[1, sec], device_id=(far, me), device_id_type=MESH
        ).start()

    @pl.when(chip == 1)
    def _():
        rsum[me] = rown[...]

        def send_sum(i, _):
            p = lax.rem(me + 1 + i, PEERS)
            pltpu.make_async_remote_copy(
                rown, rsum.at[me], rssem, rsem, device_id=(sec, p), device_id_type=MESH
            ).start()
            return 0

        lax.fori_loop(0, PEERS - 1, send_sum, 0)

    w_up_far = pltpu.make_async_remote_copy(
        up_hbm, wup.at[core], wssem.at[0], wsem.at[core, 0], device_id=(other, me), device_id_type=MESH
    )
    w_dn_far = pltpu.make_async_remote_copy(
        dn_hbm, wdn.at[core], wssem.at[1], wsem.at[core, 1], device_id=(other, me), device_id_type=MESH
    )
    w_up_far.start()
    w_dn_far.start()

    def tables_in(n, _):
        pltpu.make_async_copy(itv.at[n], itv.at[n], tsem.at[0, n]).wait()
        pltpu.make_async_copy(ftv.at[n], ftv.at[n], tsem.at[1, n]).wait()
        return 0

    lax.fori_loop(0, 4, tables_in, 0)
    c1 = pltpu.make_async_copy(itv, its, ssem_t.at[0])
    c2 = pltpu.make_async_copy(ftv, fts, ssem_t.at[1])
    c1.start()
    c2.start()
    c1.wait()
    c2.wait()

    def wait_weights(q):
        pltpu.make_async_copy(wup.at[q], wup.at[q], wsem.at[q, 0]).wait()
        pltpu.make_async_copy(wdn.at[q], wdn.at[q], wsem.at[q, 1]).wait()

    def dispatch(j, layer, recv, sem, scaled):
        here = layer // 2 == chip
        target = (layer // 2) * 2 + core
        unit = lax.rem(layer, 2) * OWN + j
        m = 2 * j + core

        def one(i, _):
            p = lax.rem(me + 1 + i, PEERS)
            for r in range(CAP):
                at = PAIRS + p * CAP + r
                row = nrm[its[layer, m, at]]
                if scaled:
                    row = (row.astype(F32) * fts[layer, m, at]).astype(BF)
                send_a[j, p, r] = row

            @pl.when(jnp.logical_not(jnp.logical_and(here, p == me)))
            def _():
                pltpu.make_async_remote_copy(
                    send_a.at[j, p], recv.at[unit, me], ssa.at[j], sem.at[unit],
                    device_id=(target, p), device_id_type=MESH,
                ).start()

            return 0

        lax.fori_loop(0, PEERS, one, 0)

        @pl.when(here)
        def _():
            recv[unit, me] = send_a[j, me]

    def wait_blocks(buffer, sem, far):
        most = buffer.at[pl.ds(0, PEERS - 1)]
        if far is False:
            pltpu.make_async_copy(most, most, sem).wait()
            return

        @pl.when(far)
        def _():
            pltpu.make_async_copy(buffer, buffer, sem).wait()

        @pl.when(jnp.logical_not(far))
        def _():
            pltpu.make_async_copy(most, most, sem).wait()

    def wait_dispatch(j, far):
        wait_blocks(send_a.at[j], ssa.at[j], far)

    def normed(value):
        v = value.astype(F32)
        mean = jnp.sum(v * v, axis=(0, 1), keepdims=True) * (1.0 / D)
        return (v * lax.rsqrt(mean + EPS)).astype(BF)

    def blocks_in(j, to, slot):
        pltpu.make_async_copy(inbuf.at[j], inbuf.at[j], insem.at[j]).wait()
        for b in range(SUB):
            lay[pl.ds(b, TOK, stride=SUB), :] = inbuf[j, :, pl.ds(b * 128, 128)].astype(F32)
        to[j, slot] = lay[pl.ds(0, TOK * SUB), :].reshape(TOK, SUB, 128).astype(BF)

    def blocks_out(kind, j, q):
        for b in range(SUB):
            outbuf[kind, q * OWN + j, :, pl.ds(b * 128, 128)] = lay[pl.ds(b, TOK, stride=SUB), :].astype(BF)

    def first_forward(j):
        blocks_in(j, xbuf, 0)

        def one(t, _):
            nrm[t] = normed(xbuf[j, 0, t])
            return 0

        lax.fori_loop(0, TOK, one, 0, unroll=4)
        dispatch(j, 0, recv_a, asem, False)

    def first_backward(j):
        blocks_in(j, gbuf, 2)
        total = jnp.sum(rsum[...], axis=0)
        inverse = (MICRO * TOK * PEERS) / total
        m = 2 * j + core

        def one(t, _):
            factor = rw[m, t] * inverse[0:1, :]
            g = (gbuf[j, 2, t].astype(F32) * factor).astype(BF)
            gbuf[j, 2, t] = g
            nrm[t] = g
            return 0

        lax.fori_loop(0, TOK, one, 0, unroll=4)
        dispatch(j, 3, recv_d, dsem, True)

    @pl.when(chip == 1)
    def _():
        most = rsum.at[pl.ds(0, PEERS - 1)]
        pltpu.make_async_copy(most, most, rsem).wait()
        pltpu.make_async_copy(most, most, rssem).wait()

    def flatten(recv, unit, dst, *lead):
        for n in range(PEERS):
            lay[pl.ds(n * CAP * SUB, CAP * SUB), :] = (
                recv[unit, n].astype(F32).reshape(CAP * SUB, 128)
            )
        for n in range(ROWS // SUB):
            for b in range(SUB):
                part = lay[pl.ds(n * SUB * SUB + b, SUB, stride=SUB), :]
                if lead:
                    q, start = lead
                    dst[q, pl.ds(pl.multiple_of(start + n * SUB, SUB), SUB), pl.ds(b * 128, 128)] = part.astype(BF)
                else:
                    dst[pl.ds(n * SUB, SUB), pl.ds(b * 128, 128)] = part.astype(BF)

    def put_back(n, tile):
        for h in range(2):
            lay[pl.ds(2 * n + h, ROWS, stride=SUB), :] = tile[:, h * 128:(h + 1) * 128]

    def give_back(j, unit, recv, sem, again):
        @pl.when(again)
        def _():
            wait_blocks(send_b.at[j], ssb.at[j], False)

        def one(i, _):
            p = lax.rem(me + 1 + i, PEERS)
            at = pl.multiple_of(p * (CAP * SUB), CAP * SUB)
            send_b[j, p] = lay[pl.ds(at, CAP * SUB), :].reshape(CAP, SUB, 128).astype(BF)

            @pl.when(p != me)
            def _():
                pltpu.make_async_remote_copy(
                    send_b.at[j, p], recv.at[unit, me], ssb.at[j], sem.at[unit],
                    device_id=(sec, p), device_id_type=MESH,
                ).start()

            return 0

        lax.fori_loop(0, PEERS, one, 0)
        recv[unit, me] = send_b[j, me]

    def expert_forward(j, q):
        unit = q * OWN + j
        start = pl.multiple_of(j * ROWS, ROWS)
        wait_blocks(recv_a.at[unit], asem.at[unit], jnp.logical_and(chip == 1, q == 0))
        flatten(recv_a, unit, rows, q, start)
        span = pl.ds(start, ROWS)
        for n in range(FF // 256):
            cols = pl.ds(n * 256, 256)
            v = jnp.dot(rows[q, span, :], wup[q, :, cols], preferred_element_type=F32)
            pre[q, span, cols] = v
            act[:, cols] = (v * jax.nn.sigmoid(v)).astype(BF)
        for n in range(D // 256):
            put_back(n, jnp.dot(act[...], wdn[q, :, pl.ds(n * 256, 256)], preferred_element_type=F32))
        give_back(j, unit, recv_b, bsem, q == 1)

    contract_last = (((1,), (1,)), ((), ()))

    def expert_backward(j, q):
        unit = q * OWN + j
        start = pl.multiple_of(j * ROWS, ROWS)
        wait_blocks(recv_d.at[unit], dsem.at[unit], jnp.logical_and(chip == 0, q == 1))
        flatten(recv_d, unit, gb)
        span = pl.ds(start, ROWS)
        for n in range(FF // 256):
            cols = pl.ds(n * 256, 256)
            v = lax.dot_general(gb[...], wdn[q, cols, :], contract_last, preferred_element_type=F32)
            h = pre[q, span, cols]
            s = jax.nn.sigmoid(h)
            gp[q, span, cols] = (v * (s * (1.0 + h * (1.0 - s)))).astype(BF)
        for n in range(D // 256):
            put_back(
                n,
                lax.dot_general(
                    gp[q, span, :], wup[q, pl.ds(n * 256, 256), :], contract_last, preferred_element_type=F32
                ),
            )
        give_back(j, unit, recv_e, esem, q < 2)

    def copy_out(kind, j, q, dst_hbm):
        m = 2 * j + core
        blocks_out(kind, j, q)
        src = outbuf.at[kind, q * OWN + j]

        @pl.when(q == core)
        def _():
            pltpu.make_async_copy(src, dst_hbm.at[m], osem.at[kind, j]).start()

        @pl.when(q != core)
        def _():
            pltpu.make_async_remote_copy(
                src, dst_hbm.at[m], ossem.at[kind, j], orsem.at[kind, j],
                device_id=(other, me), device_id_type=MESH,
            ).start()

    def home_forward(j, q):
        unit = q * OWN + j
        layer = 2 * chip + q
        m = 2 * j + core

        @pl.when(jnp.logical_and(chip == 1, q == 0))
        def _():
            pltpu.make_async_copy(xbuf.at[j, 0], xbuf.at[j, 0], xsem.at[j]).wait()

        wait_blocks(recv_b.at[unit], bsem.at[unit], False)
        work[...] = recv_b[unit].reshape(ROWS, SUB, 128)

        def one(t, _):
            total = xbuf[j, q, t].astype(F32)
            for n in range(TOP):
                total += fts[layer, m, t * TOP + n] * work[its[layer, m, t * TOP + n]].astype(F32)
            out = total.astype(BF)
            xbuf[j, q + 1, t] = out
            lay[pl.ds(pl.multiple_of(t * SUB, SUB), SUB), :] = out.astype(F32)
            nrm[t] = normed(out)
            return 0

        lax.fori_loop(0, TOK, one, 0, unroll=4)

        @pl.when(jnp.logical_not(jnp.logical_and(chip == 1, q == 1)))
        def _():
            wait_dispatch(j, False)
            dispatch(j, layer + 1, recv_a, asem, False)

        @pl.when(jnp.logical_and(chip == 0, q == 1))
        def _():
            pltpu.make_async_remote_copy(
                xbuf.at[j, 2], xbuf.at[j, 0], xs.at[j], xsem.at[j],
                device_id=(across, me), device_id_type=MESH,
            ).start()

        copy_out(0, j, q, lo_hbm)

    def home_backward(j, q):
        unit = q * OWN + j
        layer = 2 * chip + q
        m = 2 * j + core

        @pl.when(jnp.logical_and(chip == 0, q == 1))
        def _():
            pltpu.make_async_copy(gbuf.at[j, 2], gbuf.at[j, 2], gsem.at[j]).wait()

        wait_blocks(recv_e.at[unit], esem.at[unit], False)
        work[...] = recv_e[unit].reshape(ROWS, SUB, 128)

        def one(t, _):
            grad = work[its[layer, m, t * TOP]].astype(F32)
            for n in range(1, TOP):
                grad += work[its[layer, m, t * TOP + n]].astype(F32)
            x = xbuf[j, q, t].astype(F32)
            scale = lax.rsqrt(jnp.sum(x * x, axis=(0, 1), keepdims=True) * (1.0 / D) + EPS)
            inner = jnp.sum(grad * x, axis=(0, 1), keepdims=True) * (1.0 / D)
            g = gbuf[j, q + 1, t].astype(F32)
            out = (g + (scale * grad - x * (scale * scale * scale) * inner)).astype(BF)
            gbuf[j, q, t] = out
            nrm[t] = out
            lay[pl.ds(pl.multiple_of(t * SUB, SUB), SUB), :] = out.astype(F32)
            return 0

        lax.fori_loop(0, TOK, one, 0, unroll=4)

        @pl.when(jnp.logical_not(jnp.logical_and(chip == 0, q == 0)))
        def _():
            wait_dispatch(j, chip == 0)
            dispatch(j, layer - 1, recv_d, dsem, True)

        @pl.when(jnp.logical_and(chip == 1, q == 0))
        def _():
            pltpu.make_async_remote_copy(
                gbuf.at[j, 0], gbuf.at[j, 2], xs.at[j], gsem.at[j],
                device_id=(across, me), device_id_type=MESH,
            ).start()

        copy_out(1, j, q, ig_hbm)

    def weight_grad(q):
        def one(n, _):
            at = pl.multiple_of(n * 256, 256)
            gpart[q, pl.ds(at, 256), :] = lax.dot_general(
                rows[q, :, pl.ds(at, 256)], gp[q], (((0,), (0,)), ((), ())), preferred_element_type=F32
            ).astype(BF)
            return 0

        lax.fori_loop(0, D // 256, one, 0)

        @pl.when(q == core)
        def _():
            pltpu.make_async_copy(gpart.at[q], own_hbm, gusem.at[1]).start()

        @pl.when(q != core)
        def _():
            pltpu.make_async_remote_copy(
                gpart.at[q], far_hbm, gssem, gusem.at[0], device_id=(other, me), device_id_type=MESH
            ).start()

    def step(at, _):
        code = 0
        for n, (a, b) in enumerate(zip(ORDER[0], ORDER[1], strict=True)):
            code = jnp.where(at == n, jnp.where(chip == 0, a, b), code)
        kind = code // 8
        q = lax.rem(code, 8) // OWN
        j = lax.rem(code, OWN)

        @pl.when(jnp.logical_and(kind == FIRST, chip == 0))
        def _():
            first_forward(j)

        @pl.when(jnp.logical_and(kind == FIRST, chip == 1))
        def _():
            first_backward(j)

        for name, work_of in (
            (EXPERT_F, expert_forward),
            (HOME_F, home_forward),
            (EXPERT_B, expert_backward),
            (HOME_B, home_backward),
        ):
            pl.when(kind == name)(functools.partial(work_of, j, q))
        pl.when(kind == GRAD)(functools.partial(weight_grad, q))
        pl.when(kind == WEIGHTS)(functools.partial(wait_weights, q))
        return 0

    lax.fori_loop(0, len(ORDER[0]), step, 0)

    def drain(j, _):
        wait_dispatch(j, chip == 1)
        pltpu.make_async_copy(xbuf.at[j, 0], xbuf.at[j, 0], xs.at[j]).wait()
        for kind in range(2):
            for sem in (osem, orsem, ossem):
                pltpu.make_async_copy(outbuf.at[0, 0], outbuf.at[0, 0], sem.at[kind, j]).wait()
        wait_blocks(send_b.at[j], ssb.at[j], False)
        return 0

    lax.fori_loop(0, OWN, drain, 0)
    for sem in (gusem.at[0], gusem.at[1], gssem):
        pltpu.make_async_copy(gpart.at[0], gpart.at[0], sem).wait()
    w_up_far.wait_send()
    w_dn_far.wait_send()
    for n in range(3):
        pltpu.make_async_copy(itv.at[0], itv.at[0], tssem.at[0, n]).wait()
        pltpu.make_async_copy(ftv.at[0], ftv.at[0], tssem.at[1, n]).wait()


def tables(routes, combine):
    route = routes.reshape(MICRO, PAIRS)
    coef = combine.reshape(MICRO, PAIRS)
    place = jnp.arange(PAIRS, dtype=jnp.int32)
    same = (route[:, :, None] == route[:, None, :]) & (place[None, None, :] < place[None, :, None])
    slot = route * CAP + jnp.sum(same.astype(jnp.int32), axis=2)
    hit = slot[:, None, :] == jnp.arange(ROWS, dtype=jnp.int32)[None, :, None]
    token = jnp.sum(jnp.where(hit, (place // TOP)[None, None, :], 0), axis=2)
    weight = jnp.sum(jnp.where(hit, coef[:, None, :], 0.0), axis=2)
    rest = TAB - PAIRS - ROWS
    ints = jnp.concatenate([slot, token, jnp.zeros((MICRO, rest), jnp.int32)], axis=1)
    floats = jnp.concatenate([coef, weight, jnp.zeros((MICRO, rest), F32)], axis=1)
    return ints, floats


def shards(tokens, cotangent, reward_weight, routes, combine, w_up, w_down):
    ints, floats = tables(routes[0], combine[0])
    blocks = (MICRO, TOK, D)
    exchange = (PEERS, CAP, SUB, 128)
    anywhere = pl.BlockSpec(memory_space=pl.ANY)
    dma = pltpu.SemaphoreType.DMA
    lo, ig, own, far = pl.pallas_call(
        kernel,
        out_shape=(
            jax.ShapeDtypeStruct(blocks, BF),
            jax.ShapeDtypeStruct(blocks, BF),
            jax.ShapeDtypeStruct((D, FF), BF),
            jax.ShapeDtypeStruct((D, FF), BF),
        ),
        in_specs=[anywhere] * 6 + [pl.BlockSpec(memory_space=pltpu.VMEM), pl.BlockSpec(memory_space=pltpu.SMEM)],
        out_specs=(anywhere,) * 4,
        scratch_shapes=[
            pltpu.VMEM((2, D, FF), BF),
            pltpu.VMEM((2, FF, D), BF),
            pltpu.VMEM((2, OWN * ROWS, D), BF),
            pltpu.VMEM((2, OWN * ROWS, FF), F32),
            pltpu.VMEM((2, OWN * ROWS, FF), BF),
            pltpu.VMEM((2 * OWN,) + exchange, BF),
            pltpu.VMEM((2 * OWN,) + exchange, BF),
            pltpu.VMEM((2 * OWN,) + exchange, BF),
            pltpu.VMEM((2 * OWN,) + exchange, BF),
            pltpu.VMEM((OWN,) + exchange, BF),
            pltpu.VMEM((OWN,) + exchange, BF),
            pltpu.VMEM((ROWS, SUB, 128), BF),
            pltpu.VMEM((TOK, SUB, 128), BF),
            pltpu.VMEM((ROWS, D), BF),
            pltpu.VMEM((ROWS, FF), BF),
            pltpu.VMEM((ROWS * SUB, 128), F32),
            pltpu.VMEM((2, D, FF), BF),
            pltpu.VMEM((OWN, TOK, D), BF),
            pltpu.VMEM((2, 2 * OWN, TOK, D), BF),
            pltpu.VMEM((OWN, 3, TOK, SUB, 128), BF),
            pltpu.VMEM((OWN, 3, TOK, SUB, 128), BF),
            pltpu.VMEM((4, MICRO, TAB), jnp.int32),
            pltpu.VMEM((4, MICRO, TAB), F32),
            pltpu.SMEM((4, MICRO, TAB), jnp.int32),
            pltpu.SMEM((4, MICRO, TAB), F32),
            pltpu.VMEM((PEERS, 8, 128), F32),
            pltpu.VMEM((8, 128), F32),
            dma((2, 2)), dma((2,)), dma((2, 4)), dma((2, 3)), dma((2,)), dma, dma,
            dma((2 * OWN,)), dma((2 * OWN,)), dma((2 * OWN,)), dma((2 * OWN,)), dma((OWN,)), dma((OWN,)),
            dma((OWN,)), dma((OWN,)), dma((OWN,)), dma((OWN,)),
            dma((2, OWN)), dma((2, OWN)), dma((2, OWN)), dma((2,)), dma,
        ],
        compiler_params=pltpu.CompilerParams(
            collective_id=0, has_side_effects=True, vmem_limit_bytes=63 * 1024 * 1024
        ),
        cost_estimate=pl.CostEstimate(
            flops=2 * 5 * MICRO * ROWS * D * FF, bytes_accessed=16 * 2**20, transcendentals=2 * MICRO * ROWS * FF
        ),
    )(
        tokens, cotangent, w_up[0, 0], w_down[0, 0], ints, floats, reward_weight, reward_weight
    )
    grad = (own.astype(F32) + far.astype(F32)).astype(BF)
    return lo[None], ig[None], grad[None, None]


def solution(mesh):
    return jax.shard_map(
        shards,
        mesh=mesh,
        in_specs=(
            P(None, "expert", None),
            P(None, "expert", None),
            P(None, "expert"),
            P("section", None, "expert", None),
            P("section", None, "expert", None),
            P("section", "expert", None, None),
            P("section", "expert", None, None),
        ),
        out_specs=(
            P("section", None, "expert", None),
            P("section", None, "expert", None),
            P("section", "expert", None, None),
        ),
        check_vma=False,
    )
```

```python
import functools

import jax
import jax.numpy as jnp
from jax import lax
from jax.experimental import pallas as pl
from jax.experimental.pallas import tpu as pltpu
from jax.sharding import PartitionSpec as P

EPS = 1e-06
MESH = pl.DeviceIdType.MESH
BF = jnp.bfloat16
F32 = jnp.float32

PEERS = 32
CAP = 5
ROWS = PEERS * CAP
TOK = 16
TOP = 8
MICRO = 8
OWN = 4
D = 2048
FF = 768
SUB = 16
PAIRS = TOK * TOP
TAB = 384

FIRST, EXPERT_F, HOME_F, EXPERT_B, HOME_B, GRAD, WEIGHTS = range(7)


def steps(*words):
    names = {"I": FIRST, "X": EXPERT_F, "H": HOME_F, "Y": EXPERT_B, "G": HOME_B, "U": GRAD, "W": WEIGHTS}
    return [names[w[0]] * 8 + int(w[2]) * OWN + int(w[1]) for w in words]


ORDER = (
    steps(
        "I00", "I20", "I10", "W00", "X00", "X10", "H00", "H10", "W01", "X01",
        "X11", "H01", "H11", "I30", "X30", "X20", "H30", "H20", "X31", "X21",
        "H31", "H21", "Y11", "Y01", "G11", "G01", "Y10", "Y00", "G10", "G00",
        "Y31", "Y21", "G31", "U01", "G21", "Y30", "Y20", "U00", "G30", "G20",
    ),
    steps(
        "I30", "I20", "I10", "I00", "W00", "X00", "X10", "H00", "H10", "W01",
        "X01", "Y01", "X11", "Y11", "G01", "G11", "Y00", "X30", "X20", "Y10",
        "H30", "H20", "G10", "G00", "H11", "X31", "Y31", "X21", "Y21", "U01",
        "H31", "G31", "G21", "Y30", "Y20", "G30", "H01", "G20", "U00", "H21",
    ),
)


def offset(n):
    return jnp.where(n == 0, 2, jnp.where(n == 1, 1, jnp.where(n == 2, 3, 0)))


def kernel(
    tok_hbm, cot_hbm, up_hbm, dn_hbm, it_hbm, ft_hbm, rv, rw,
    lo_hbm, ig_hbm, own_hbm, far_hbm,
    wup, wdn, rows, pre, gp, recv_a, recv_b, recv_d, recv_e, send_a, send_b, work, nrm, gb, act, lay,
    gpart, inbuf, outbuf, xbuf, gbuf, itv, ftv, its, fts, rsum, rown,
    wsem, wssem, tsem, tssem, ssem_t, rsem, rssem, asem, bsem, dsem, esem, ssa, ssb,
    insem, xsem, gsem, xs, osem, orsem, ossem, gusem, gssem,
):
    sec = lax.axis_index("section")
    me = lax.axis_index("expert")
    chip = sec // 2
    core = lax.rem(sec, 2)
    other = chip * 2 + (1 - core)
    across = (1 - chip) * 2 + core
    diag = (1 - chip) * 2 + (1 - core)

    def peer(i):
        y = lax.rem(me // 8 + offset(lax.rem(i // 4, 4)), 4)
        z = lax.rem(me // 4 + 1 - i // 16, 2)
        x = lax.rem(me + offset(lax.rem(i, 4)), 4)
        return y * 8 + z * 4 + x

    pltpu.make_async_copy(up_hbm, wup.at[core], wsem.at[core, 0]).start()
    pltpu.make_async_copy(dn_hbm, wdn.at[core], wsem.at[core, 1]).start()
    pltpu.make_async_copy(it_hbm, itv.at[sec], tsem.at[0, sec]).start()
    pltpu.make_async_copy(ft_hbm, ftv.at[sec], tsem.at[1, sec]).start()

    def load_tokens(j, _):
        @pl.when(chip == 0)
        def _():
            pltpu.make_async_copy(tok_hbm.at[2 * j + core], inbuf.at[j], insem.at[j]).start()

        @pl.when(chip == 1)
        def _():
            pltpu.make_async_copy(cot_hbm.at[2 * j + core], inbuf.at[j], insem.at[j]).start()

        return 0

    lax.fori_loop(0, OWN, load_tokens, 0)

    rown[...] = jnp.broadcast_to(jnp.sum(rv[...], axis=(0, 1), keepdims=True), (8, 128))

    barrier = pltpu.get_barrier_semaphore()

    def greet(i, _):
        p = lax.rem(me + 1 + i, PEERS)

        pl.semaphore_signal(barrier, inc=1, device_id=(sec, p), device_id_type=MESH)
        return 0

    for far in (across, diag, other):
        pl.semaphore_signal(barrier, inc=1, device_id=(far, me), device_id_type=MESH)
    lax.fori_loop(0, PEERS - 1, greet, 0)
    pl.semaphore_wait(barrier, PEERS + 2)

    for n, far in enumerate((other, across, diag)):
        pltpu.make_async_remote_copy(
            it_hbm, itv.at[sec], tssem.at[0, n], tsem.at[0, sec], device_id=(far, me), device_id_type=MESH
        ).start()
        pltpu.make_async_remote_copy(
            ft_hbm, ftv.at[sec], tssem.at[1, n], tsem.at[1, sec], device_id=(far, me), device_id_type=MESH
        ).start()

    w_up_far = pltpu.make_async_remote_copy(
        up_hbm, wup.at[core], wssem.at[0], wsem.at[core, 0], device_id=(other, me), device_id_type=MESH
    )
    w_dn_far = pltpu.make_async_remote_copy(
        dn_hbm, wdn.at[core], wssem.at[1], wsem.at[core, 1], device_id=(other, me), device_id_type=MESH
    )
    w_up_far.start()
    w_dn_far.start()

    def tables_in(n, _):
        pltpu.make_async_copy(itv.at[n], itv.at[n], tsem.at[0, n]).wait()
        pltpu.make_async_copy(ftv.at[n], ftv.at[n], tsem.at[1, n]).wait()
        return 0

    lax.fori_loop(0, 4, tables_in, 0)
    c1 = pltpu.make_async_copy(itv, its, ssem_t.at[0])
    c2 = pltpu.make_async_copy(ftv, fts, ssem_t.at[1])
    c1.start()
    c2.start()
    @pl.when(chip == 1)
    def _():
        rsum[me] = rown[...]

        def send_sum(i, _):
            p = lax.rem(me + 1 + i, PEERS)
            pltpu.make_async_remote_copy(
                rown, rsum.at[me], rssem, rsem, device_id=(sec, p), device_id_type=MESH
            ).start()
            return 0

        lax.fori_loop(0, PEERS - 1, send_sum, 0)

    c1.wait()
    c2.wait()

    def wait_weights(q):
        pltpu.make_async_copy(wup.at[q], wup.at[q], wsem.at[q, 0]).wait()
        pltpu.make_async_copy(wdn.at[q], wdn.at[q], wsem.at[q, 1]).wait()

    def dispatch(j, layer, recv, sem, scaled):
        here = layer // 2 == chip
        target = (layer // 2) * 2 + core
        unit = lax.rem(layer, 2) * OWN + j
        m = 2 * j + core

        def one(i, _):
            p = lax.rem(me + 1 + i, PEERS)
            for r in range(CAP):
                at = PAIRS + p * CAP + r
                row = nrm[its[layer, m, at]]
                if scaled:
                    row = (row.astype(F32) * fts[layer, m, at]).astype(BF)
                send_a[j, p, r] = row

            @pl.when(jnp.logical_not(jnp.logical_and(here, p == me)))
            def _():
                pltpu.make_async_remote_copy(
                    send_a.at[j, p], recv.at[unit, me], ssa.at[j], sem.at[unit],
                    device_id=(target, p), device_id_type=MESH,
                ).start()

            return 0

        lax.fori_loop(0, PEERS, one, 0, unroll=4)

        @pl.when(here)
        def _():
            recv[unit, me] = send_a[j, me]

    def wait_blocks(buffer, sem, far):
        most = buffer.at[pl.ds(0, PEERS - 1)]
        if far is False:
            pltpu.make_async_copy(most, most, sem).wait()
            return

        @pl.when(far)
        def _():
            pltpu.make_async_copy(buffer, buffer, sem).wait()

        @pl.when(jnp.logical_not(far))
        def _():
            pltpu.make_async_copy(most, most, sem).wait()

    def wait_dispatch(j, far):
        wait_blocks(send_a.at[j], ssa.at[j], far)

    def normed(value):
        v = value.astype(F32)
        mean = jnp.sum(v * v, axis=(0, 1), keepdims=True) * (1.0 / D)
        return (v * lax.rsqrt(mean + EPS)).astype(BF)

    def blocks_in(j, to, slot):
        pltpu.make_async_copy(inbuf.at[j], inbuf.at[j], insem.at[j]).wait()
        for b in range(SUB):
            lay[pl.ds(b, TOK, stride=SUB), :] = inbuf[j, :, pl.ds(b * 128, 128)].astype(F32)
        to[j, slot] = lay[pl.ds(0, TOK * SUB), :].reshape(TOK, SUB, 128).astype(BF)

    def blocks_out(kind, j, q):
        for b in range(SUB):
            outbuf[kind, q * OWN + j, :, pl.ds(b * 128, 128)] = lay[pl.ds(b, TOK, stride=SUB), :].astype(BF)

    def first_forward(j):
        blocks_in(j, xbuf, 0)

        def one(t, _):
            nrm[t] = normed(xbuf[j, 0, t])
            return 0

        lax.fori_loop(0, TOK, one, 0, unroll=4)
        dispatch(j, 0, recv_a, asem, False)

    def first_backward(j):
        blocks_in(j, gbuf, 2)
        total = jnp.sum(rsum[...], axis=0)
        inverse = (MICRO * TOK * PEERS) / total
        m = 2 * j + core

        def one(t, _):
            factor = rw[m, t] * inverse[0:1, :]
            g = (gbuf[j, 2, t].astype(F32) * factor).astype(BF)
            gbuf[j, 2, t] = g
            nrm[t] = g
            return 0

        lax.fori_loop(0, TOK, one, 0, unroll=4)
        dispatch(j, 3, recv_d, dsem, True)

    @pl.when(chip == 1)
    def _():
        most = rsum.at[pl.ds(0, PEERS - 1)]
        pltpu.make_async_copy(most, most, rsem).wait()
        pltpu.make_async_copy(most, most, rssem).wait()

    def flatten(recv, unit, dst, *lead):
        for n in range(PEERS):
            lay[pl.ds(n * CAP * SUB, CAP * SUB), :] = (
                recv[unit, n].astype(F32).reshape(CAP * SUB, 128)
            )
        for n in range(ROWS // SUB):
            for b in range(SUB):
                part = lay[pl.ds(n * SUB * SUB + b, SUB, stride=SUB), :]
                if lead:
                    q, start = lead
                    dst[q, pl.ds(pl.multiple_of(start + n * SUB, SUB), SUB), pl.ds(b * 128, 128)] = part.astype(BF)
                else:
                    dst[pl.ds(n * SUB, SUB), pl.ds(b * 128, 128)] = part.astype(BF)

    def put_back(n, tile):
        for h in range(2):
            lay[pl.ds(2 * n + h, ROWS, stride=SUB), :] = tile[:, h * 128:(h + 1) * 128]

    def give_back(j, unit, recv, sem, again):
        @pl.when(again)
        def _():
            wait_blocks(send_b.at[j], ssb.at[j], False)

        def one(i, _):
            p = lax.rem(me + 1 + i, PEERS)
            at = pl.multiple_of(p * (CAP * SUB), CAP * SUB)
            send_b[j, p] = lay[pl.ds(at, CAP * SUB), :].reshape(CAP, SUB, 128).astype(BF)

            @pl.when(p != me)
            def _():
                pltpu.make_async_remote_copy(
                    send_b.at[j, p], recv.at[unit, me], ssb.at[j], sem.at[unit],
                    device_id=(sec, p), device_id_type=MESH,
                ).start()

            return 0

        lax.fori_loop(0, PEERS, one, 0, unroll=4)
        recv[unit, me] = send_b[j, me]

    def expert_forward(j, q):
        unit = q * OWN + j
        start = pl.multiple_of(j * ROWS, ROWS)
        wait_blocks(recv_a.at[unit], asem.at[unit], jnp.logical_and(chip == 1, q == 0))
        flatten(recv_a, unit, rows, q, start)
        span = pl.ds(start, ROWS)
        for n in range(FF // 256):
            cols = pl.ds(n * 256, 256)
            v = jnp.dot(rows[q, span, :], wup[q, :, cols], preferred_element_type=F32)
            pre[q, span, cols] = v
            act[:, cols] = (v * jax.nn.sigmoid(v)).astype(BF)
        for n in range(D // 256):
            put_back(n, jnp.dot(act[...], wdn[q, :, pl.ds(n * 256, 256)], preferred_element_type=F32))
        give_back(j, unit, recv_b, bsem, q == 1)

    contract_last = (((1,), (1,)), ((), ()))

    def expert_backward(j, q):
        unit = q * OWN + j
        start = pl.multiple_of(j * ROWS, ROWS)
        wait_blocks(recv_d.at[unit], dsem.at[unit], jnp.logical_and(chip == 0, q == 1))
        flatten(recv_d, unit, gb)
        span = pl.ds(start, ROWS)
        for n in range(FF // 256):
            cols = pl.ds(n * 256, 256)
            v = lax.dot_general(gb[...], wdn[q, cols, :], contract_last, preferred_element_type=F32)
            h = pre[q, span, cols]
            s = jax.nn.sigmoid(h)
            gp[q, span, cols] = (v * (s * (1.0 + h * (1.0 - s)))).astype(BF)
        for n in range(D // 256):
            put_back(
                n,
                lax.dot_general(
                    gp[q, span, :], wup[q, pl.ds(n * 256, 256), :], contract_last, preferred_element_type=F32
                ),
            )
        give_back(j, unit, recv_e, esem, q < 2)

    def copy_out(kind, j, q, dst_hbm):
        m = 2 * j + core
        blocks_out(kind, j, q)
        src = outbuf.at[kind, q * OWN + j]

        @pl.when(q == core)
        def _():
            pltpu.make_async_copy(src, dst_hbm.at[m], osem.at[kind, j]).start()

        @pl.when(q != core)
        def _():
            pltpu.make_async_remote_copy(
                src, dst_hbm.at[m], ossem.at[kind, j], orsem.at[kind, j],
                device_id=(other, me), device_id_type=MESH,
            ).start()

    def home_forward(j, q):
        unit = q * OWN + j
        layer = 2 * chip + q
        m = 2 * j + core

        @pl.when(jnp.logical_and(chip == 1, q == 0))
        def _():
            pltpu.make_async_copy(xbuf.at[j, 0], xbuf.at[j, 0], xsem.at[j]).wait()

        wait_blocks(recv_b.at[unit], bsem.at[unit], False)
        work[...] = recv_b[unit].reshape(ROWS, SUB, 128)

        def one(t, _):
            total = xbuf[j, q, t].astype(F32)
            for n in range(TOP):
                total += fts[layer, m, t * TOP + n] * work[its[layer, m, t * TOP + n]].astype(F32)
            out = total.astype(BF)
            xbuf[j, q + 1, t] = out
            lay[pl.ds(pl.multiple_of(t * SUB, SUB), SUB), :] = out.astype(F32)
            nrm[t] = normed(out)
            return 0

        lax.fori_loop(0, TOK, one, 0, unroll=4)

        @pl.when(jnp.logical_not(jnp.logical_and(chip == 1, q == 1)))
        def _():
            wait_dispatch(j, False)
            dispatch(j, layer + 1, recv_a, asem, False)

        @pl.when(jnp.logical_and(chip == 0, q == 1))
        def _():
            pltpu.make_async_remote_copy(
                xbuf.at[j, 2], xbuf.at[j, 0], xs.at[j], xsem.at[j],
                device_id=(across, me), device_id_type=MESH,
            ).start()

        copy_out(0, j, q, lo_hbm)

    def home_backward(j, q):
        unit = q * OWN + j
        layer = 2 * chip + q
        m = 2 * j + core

        @pl.when(jnp.logical_and(chip == 0, q == 1))
        def _():
            pltpu.make_async_copy(gbuf.at[j, 2], gbuf.at[j, 2], gsem.at[j]).wait()

        wait_blocks(recv_e.at[unit], esem.at[unit], False)
        work[...] = recv_e[unit].reshape(ROWS, SUB, 128)

        def one(t, _):
            grad = work[its[layer, m, t * TOP]].astype(F32)
            for n in range(1, TOP):
                grad += work[its[layer, m, t * TOP + n]].astype(F32)
            x = xbuf[j, q, t].astype(F32)
            scale = lax.rsqrt(jnp.sum(x * x, axis=(0, 1), keepdims=True) * (1.0 / D) + EPS)
            inner = jnp.sum(grad * x, axis=(0, 1), keepdims=True) * (1.0 / D)
            g = gbuf[j, q + 1, t].astype(F32)
            out = (g + (scale * grad - x * (scale * scale * scale) * inner)).astype(BF)
            gbuf[j, q, t] = out
            nrm[t] = out
            lay[pl.ds(pl.multiple_of(t * SUB, SUB), SUB), :] = out.astype(F32)
            return 0

        lax.fori_loop(0, TOK, one, 0, unroll=4)

        @pl.when(jnp.logical_not(jnp.logical_and(chip == 0, q == 0)))
        def _():
            wait_dispatch(j, chip == 0)
            dispatch(j, layer - 1, recv_d, dsem, True)

        @pl.when(jnp.logical_and(chip == 1, q == 0))
        def _():
            pltpu.make_async_remote_copy(
                gbuf.at[j, 0], gbuf.at[j, 2], xs.at[j], gsem.at[j],
                device_id=(across, me), device_id_type=MESH,
            ).start()

        copy_out(1, j, q, ig_hbm)

    def weight_grad(q):
        def one(n, _):
            at = pl.multiple_of(n * 256, 256)
            gpart[q, pl.ds(at, 256), :] = lax.dot_general(
                rows[q, :, pl.ds(at, 256)], gp[q], (((0,), (0,)), ((), ())), preferred_element_type=F32
            ).astype(BF)
            return 0

        lax.fori_loop(0, D // 256, one, 0)

        @pl.when(q == core)
        def _():
            pltpu.make_async_copy(gpart.at[q], own_hbm, gusem.at[1]).start()

        @pl.when(q != core)
        def _():
            pltpu.make_async_remote_copy(
                gpart.at[q], far_hbm, gssem, gusem.at[0], device_id=(other, me), device_id_type=MESH
            ).start()

    def step(at, _):
        code = 0
        for n, (a, b) in enumerate(zip(ORDER[0], ORDER[1], strict=True)):
            code = jnp.where(at == n, jnp.where(chip == 0, a, b), code)
        kind = code // 8
        q = lax.rem(code, 8) // OWN
        j = lax.rem(code, OWN)

        @pl.when(jnp.logical_and(kind == FIRST, chip == 0))
        def _():
            first_forward(j)

        @pl.when(jnp.logical_and(kind == FIRST, chip == 1))
        def _():
            first_backward(j)

        for name, work_of in (
            (EXPERT_F, expert_forward),
            (HOME_F, home_forward),
            (EXPERT_B, expert_backward),
            (HOME_B, home_backward),
        ):
            pl.when(kind == name)(functools.partial(work_of, j, q))
        pl.when(kind == GRAD)(functools.partial(weight_grad, q))
        pl.when(kind == WEIGHTS)(functools.partial(wait_weights, q))
        return 0

    lax.fori_loop(0, len(ORDER[0]), step, 0)

    def drain(j, _):
        wait_dispatch(j, chip == 1)
        pltpu.make_async_copy(xbuf.at[j, 0], xbuf.at[j, 0], xs.at[j]).wait()
        for kind in range(2):
            for sem in (osem, orsem, ossem):
                pltpu.make_async_copy(outbuf.at[0, 0], outbuf.at[0, 0], sem.at[kind, j]).wait()
        wait_blocks(send_b.at[j], ssb.at[j], False)
        return 0

    lax.fori_loop(0, OWN, drain, 0)
    for sem in (gusem.at[0], gusem.at[1], gssem):
        pltpu.make_async_copy(gpart.at[0], gpart.at[0], sem).wait()
    w_up_far.wait_send()
    w_dn_far.wait_send()
    for n in range(3):
        pltpu.make_async_copy(itv.at[0], itv.at[0], tssem.at[0, n]).wait()
        pltpu.make_async_copy(ftv.at[0], ftv.at[0], tssem.at[1, n]).wait()


def tables(routes, combine):
    route = routes.reshape(MICRO, PAIRS)
    coef = combine.reshape(MICRO, PAIRS)
    place = jnp.arange(PAIRS, dtype=jnp.int32)
    same = (route[:, :, None] == route[:, None, :]) & (place[None, None, :] < place[None, :, None])
    slot = route * CAP + jnp.sum(same.astype(jnp.int32), axis=2)
    hit = slot[:, None, :] == jnp.arange(ROWS, dtype=jnp.int32)[None, :, None]
    token = jnp.sum(jnp.where(hit, (place // TOP)[None, None, :], 0), axis=2)
    weight = jnp.sum(jnp.where(hit, coef[:, None, :], 0.0), axis=2)
    rest = TAB - PAIRS - ROWS
    ints = jnp.concatenate([slot, token, jnp.zeros((MICRO, rest), jnp.int32)], axis=1)
    floats = jnp.concatenate([coef, weight, jnp.zeros((MICRO, rest), F32)], axis=1)
    return ints, floats


def shards(tokens, cotangent, reward_weight, routes, combine, w_up, w_down):
    ints, floats = tables(routes[0], combine[0])
    blocks = (MICRO, TOK, D)
    exchange = (PEERS, CAP, SUB, 128)
    anywhere = pl.BlockSpec(memory_space=pl.ANY)
    dma = pltpu.SemaphoreType.DMA
    lo, ig, own, far = pl.pallas_call(
        kernel,
        out_shape=(
            jax.ShapeDtypeStruct(blocks, BF),
            jax.ShapeDtypeStruct(blocks, BF),
            jax.ShapeDtypeStruct((D, FF), BF),
            jax.ShapeDtypeStruct((D, FF), BF),
        ),
        in_specs=[anywhere] * 6 + [pl.BlockSpec(memory_space=pltpu.VMEM), pl.BlockSpec(memory_space=pltpu.SMEM)],
        out_specs=(anywhere,) * 4,
        scratch_shapes=[
            pltpu.VMEM((2, D, FF), BF),
            pltpu.VMEM((2, FF, D), BF),
            pltpu.VMEM((2, OWN * ROWS, D), BF),
            pltpu.VMEM((2, OWN * ROWS, FF), F32),
            pltpu.VMEM((2, OWN * ROWS, FF), BF),
            pltpu.VMEM((2 * OWN,) + exchange, BF),
            pltpu.VMEM((2 * OWN,) + exchange, BF),
            pltpu.VMEM((2 * OWN,) + exchange, BF),
            pltpu.VMEM((2 * OWN,) + exchange, BF),
            pltpu.VMEM((OWN,) + exchange, BF),
            pltpu.VMEM((OWN,) + exchange, BF),
            pltpu.VMEM((ROWS, SUB, 128), BF),
            pltpu.VMEM((TOK, SUB, 128), BF),
            pltpu.VMEM((ROWS, D), BF),
            pltpu.VMEM((ROWS, FF), BF),
            pltpu.VMEM((ROWS * SUB, 128), F32),
            pltpu.VMEM((2, D, FF), BF),
            pltpu.VMEM((OWN, TOK, D), BF),
            pltpu.VMEM((2, 2 * OWN, TOK, D), BF),
            pltpu.VMEM((OWN, 3, TOK, SUB, 128), BF),
            pltpu.VMEM((OWN, 3, TOK, SUB, 128), BF),
            pltpu.VMEM((4, MICRO, TAB), jnp.int32),
            pltpu.VMEM((4, MICRO, TAB), F32),
            pltpu.SMEM((4, MICRO, TAB), jnp.int32),
            pltpu.SMEM((4, MICRO, TAB), F32),
            pltpu.VMEM((PEERS, 8, 128), F32),
            pltpu.VMEM((8, 128), F32),
            dma((2, 2)), dma((2,)), dma((2, 4)), dma((2, 3)), dma((2,)), dma, dma,
            dma((2 * OWN,)), dma((2 * OWN,)), dma((2 * OWN,)), dma((2 * OWN,)), dma((OWN,)), dma((OWN,)),
            dma((OWN,)), dma((OWN,)), dma((OWN,)), dma((OWN,)),
            dma((2, OWN)), dma((2, OWN)), dma((2, OWN)), dma((2,)), dma,
        ],
        compiler_params=pltpu.CompilerParams(
            collective_id=0, has_side_effects=True, vmem_limit_bytes=63 * 1024 * 1024
        ),
        cost_estimate=pl.CostEstimate(
            flops=2 * 5 * MICRO * ROWS * D * FF, bytes_accessed=16 * 2**20, transcendentals=2 * MICRO * ROWS * FF
        ),
    )(
        tokens, cotangent, w_up[0, 0], w_down[0, 0], ints, floats, reward_weight, reward_weight
    )
    grad = (own.astype(F32) + far.astype(F32)).astype(BF)
    return lo[None], ig[None], grad[None, None]


def solution(mesh):
    return jax.shard_map(
        shards,
        mesh=mesh,
        in_specs=(
            P(None, "expert", None),
            P(None, "expert", None),
            P(None, "expert"),
            P("section", None, "expert", None),
            P("section", None, "expert", None),
            P("section", "expert", None, None),
            P("section", "expert", None, None),
        ),
        out_specs=(
            P("section", None, "expert", None),
            P("section", None, "expert", None),
            P("section", "expert", None, None),
        ),
        check_vma=False,
    )
```
